256 devices in a mesh: row: 8 (over z), col: 8 (over y_lo, x), depth: 4 (over y_hi, core).
Axes of the slice: x: 4, y: 4 (y_hi: 2, y_lo: 2; y = y_hi * 2 + y_lo), z: 8, core: 2. Of those that a mesh axis runs over, the one named last changes fastest.
Arguments:
- tokens: bfloat16 [4096, 6144], P(('depth', 'col'), 'row'), may hold values from -6 to 6
- up_weight: bfloat16 [6144, 24576], P('row', 'col'), may hold values from -0.078125 to 0.078125
- grad_out: bfloat16 [4096, 24576], P(('depth', 'row'), 'col'), may hold values from -6 to 6
Outputs:
- activated: bfloat16 [4096, 24576], P(('depth', 'row'), 'col')
- grad_tokens: bfloat16 [4096, 6144], P(('depth', 'col'), 'row')
- grad_weight: bfloat16 [6144, 24576], P('row', ('col', 'depth'))
The draws below stay inside these ranges and needn't reach their ends.
All inputs are finite; a program needn't handle non-finite values.
Results may differ from the reference program's by a relative error of at most 0.005.
Values may be sent and summed in bfloat16 or wider, within the bound.
No kernel may reach another device: no remote copies, remote signals or barrier semaphores. Data moves between devices by JAX's collectives and lax.ppermute only.
A program may use at most 128 MiB of HBM per device.

```python
import jax
import jax.numpy as jnp
from jax import lax

D = 6144
FF = 24576
TOKENS = 4096


def shard_levels(stream_key, dims, split, least, largest):
    def one(position, shards_of):
        draws = jax.random.uniform(jax.random.fold_in(jax.random.fold_in(stream_key, 6), position), (shards_of,), jnp.float32, least / len(split), largest / len(split))
        return jnp.repeat(jnp.exp(draws), dims[position] // shards_of).reshape((-1,) + (1,) * (len(dims) - position - 1))

    loudness = one(*split[0])
    for cut in split[1:]:
        loudness = loudness * one(*cut)
    return loudness


def noise(stream_key, extent, spread, most, pieces=(), dtype=jnp.bfloat16):
    array = jax.random.normal(stream_key, extent, jnp.float32) * spread
    if len(pieces) > 0:
        array = shard_levels(stream_key, extent, pieces, -0.22, 0.18) * array
    return jnp.clip(array, min=-most, max=most).astype(dtype)


def setup_inputs(seed: int = 0) -> dict:
    streams_of = jax.random.split(jax.random.key(seed), 4)
    tokens = noise(streams_of[0], (TOKENS, D), 1.0, 6.0, ((0, 32), (1, 8)))
    up_weight = noise(streams_of[1], (D, FF), D ** -0.5, 0.078125, ((0, 8), (1, 8)))
    grad_out = noise(streams_of[2], (TOKENS, FF), 1.0, 6.0, ((0, 32), (1, 8)))
    return {"tokens": tokens, "up_weight": up_weight, "grad_out": grad_out}


coeff = 0.7978845608
cubic = 0.044715


def gelu_value(hidden):
    inner = jnp.tanh(coeff * (hidden + cubic * hidden * hidden * hidden))
    return 0.5 * hidden * (1.0 + inner)


def gelu_slope(hidden):
    inner = jnp.tanh(coeff * (hidden + cubic * hidden * hidden * hidden))
    return 0.5 * (1.0 + inner) + 0.5 * hidden * (1.0 - inner * inner) * coeff * (1.0 + 3.0 * cubic * hidden * hidden)


def reference(tokens, up_weight, grad_out):
    wide_tokens = tokens.astype(jnp.float32)
    wide_weight = up_weight.astype(jnp.float32)
    hidden = jnp.dot(wide_tokens, wide_weight, precision=lax.Precision.HIGHEST)
    activated = gelu_value(hidden).astype(jnp.bfloat16)
    grad_hidden = (grad_out.astype(jnp.float32) * gelu_slope(hidden)).astype(jnp.bfloat16)
    grad_wide = grad_hidden.astype(jnp.float32)
    grad_tokens = jnp.dot(grad_wide, wide_weight.T, precision=lax.Precision.HIGHEST).astype(jnp.bfloat16)
    grad_weight = jnp.dot(wide_tokens.T, grad_wide, precision=lax.Precision.HIGHEST).astype(jnp.bfloat16)
    return activated, grad_tokens, grad_weight
```

```python
import jax
import jax.numpy as jnp
from jax import lax
from jax.sharding import PartitionSpec as P

coeff = 0.7978845608
cubic = 0.044715
HALVES = 2
STREAMS = 2


def gelu_both(hidden):
    square = hidden * hidden
    inner = jnp.tanh(coeff * (hidden + cubic * hidden * square))
    value = 0.5 * hidden * (1.0 + inner)
    slope = 0.5 * (1.0 + inner) + 0.5 * hidden * (1.0 - inner * inner) * coeff * (
        1.0 + 3.0 * cubic * square
    )
    return value, slope


def shift(x, axis, n, k):
    return lax.ppermute(x, axis, [(i, (i + k) % n) for i in range(n)])


def x_shift(x, k):
    return lax.ppermute(
        x, "col", [(y * 4 + i, y * 4 + (i + k) % 4) for y in range(2) for i in range(4)]
    )


def y_swap(x):
    return lax.ppermute(x, "col", [(i, (i + 4) % 8) for i in range(8)])


def gather_tokens(own):
    other = y_swap(own)
    out = []
    ahead = [x_shift(v, -1) for v in (own, other)]
    behind = [x_shift(v, 1) for v in (own, other)]
    far = [x_shift(ahead[0], -1), x_shift(behind[1], 1)]
    for i, v in enumerate((own, other)):
        out += [v, ahead[i], far[i], behind[i]]
    return jnp.stack(out)


def pick(panel, index):
    return lax.dynamic_index_in_dim(panel, index, 0, keepdims=False)


def on_device(tokens, up_weight, grad_out):
    f32, bf16 = jnp.float32, jnp.bfloat16
    row, col, depth = (lax.axis_index(a) for a in ("row", "col", "depth"))
    core, high = depth % 2, depth // 2
    rows = tokens.shape[0] // HALVES
    quarter = up_weight.shape[1] // 4
    piece = quarter // STREAMS

    def columns(x, j):
        return jnp.concatenate(
            [x[:, d * quarter + j * piece : d * quarter + (j + 1) * piece] for d in range(4)], 1
        )

    def place(block):
        return ((block // 4) ^ (col // 4)) * 4 + (block % 4 + 4 - col % 4) % 4

    weights = [columns(up_weight, j) for j in range(STREAMS)]
    panels = [gather_tokens(tokens[h * rows : (h + 1) * rows]) for h in range(HALVES)]

    def reduce(terms, s):
        def term(k):
            return pick(terms, place((row + k + 16) % 8))

        far = term(4 * s).astype(bf16)
        near = term(-3 * s).astype(bf16)
        for k in (3, 2, 1, 0):
            far = shift(far, "row", 8, s)
            if k:
                far = (far.astype(f32) + term(k * s)).astype(bf16)
            if k < 3:
                near = shift(near, "row", 8, -s)
                if k:
                    near = (near.astype(f32) + term(-k * s)).astype(bf16)
        return far.astype(f32) + near.astype(f32) + term(0)

    def gather(own, s):
        blocks = [own] + [None] * 7
        far = near = own
        for k in (1, 2, 3, 4):
            far = shift(far, "row", 8, s)
            blocks[(-k * s) % 8] = far
            if k < 4:
                near = shift(near, "row", 8, -s)
                blocks[(k * s) % 8] = near
        return blocks

    activated = [[None] * STREAMS for _ in range(HALVES)]
    hidden_panels = [[None] * STREAMS for _ in range(HALVES)]
    for h in range(HALVES):
        for j in range(STREAMS):
            s = 1 - 2 * (j % 2)
            terms = lax.dot_general(
                panels[h], weights[j], (((2,), (0,)), ((), ())), preferred_element_type=f32
            )
            hidden = reduce(terms, s)
            value, slope = gelu_both(hidden)
            activated[h][j] = value.astype(bf16)
            own = columns(grad_out[h * rows : (h + 1) * rows], j).astype(f32)
            hidden_panels[h][j] = gather((own * slope).astype(bf16), s)

    grad_tokens = []
    for h in range(HALVES):
        terms = sum(
            lax.dot_general(
                jnp.stack(hidden_panels[h][j]),
                weights[j],
                (((2,), (1,)), ((), ())),
                preferred_element_type=f32,
            )
            for j in range(STREAMS)
        )
        total = pick(terms, (col - row + 8) % 8)
        for k in range(1, 8):
            sent = pick(terms, (col + k - row + 8) % 8).astype(bf16)
            total = total + shift(sent, "col", 8, k).astype(f32)
        grad_tokens.append(total.astype(bf16))

    ordered = [
        jnp.concatenate([pick(panels[h], place((row + m) % 8)) for m in range(8)], 0)
        for h in range(HALVES)
    ]
    all_tokens = jnp.concatenate(ordered, 0)
    grad_weight = []
    for j in range(STREAMS):
        panel = jnp.concatenate([b for h in range(HALVES) for b in hidden_panels[h][j]], 0)

        def part(d):
            return panel[:, d * piece : (d + 1) * piece]

        def product(cols):
            return lax.dot_general(
                all_tokens, cols, (((0,), (0,)), ((), ())), preferred_element_type=f32
            )

        here = core == 0
        theirs = jnp.concatenate(
            [jnp.where(here, part(1), part(0)), jnp.where(here, part(3), part(2))], 1
        )
        low, up = jnp.where(here, part(0), part(1)), jnp.where(here, part(2), part(3))
        below = high == 0
        sent = product(theirs)
        got = lax.ppermute(sent, "depth", [(0, 1), (1, 0), (2, 3), (3, 2)])
        got_low, got_up = got[:, :piece], got[:, piece:]
        away = product(jnp.where(below, up, low)) + jnp.where(below, got_up, got_low)
        mine = product(jnp.where(below, low, up)) + jnp.where(below, got_low, got_up)
        back = lax.ppermute(away.astype(bf16), "depth", [(0, 2), (1, 3), (2, 0), (3, 1)])
        grad_weight.append((mine + back.astype(f32)).astype(bf16))

    whole = []
    for h in range(HALVES):
        parts = [
            activated[h][j][:, d * piece : (d + 1) * piece]
            for d in range(4)
            for j in range(STREAMS)
        ]
        whole.append(jnp.concatenate(parts, 1))
    return (
        jnp.concatenate(whole, 0),
        jnp.concatenate(grad_tokens, 0),
        jnp.concatenate(grad_weight, 1),
    )


def solution(mesh):
    placed = (P(("depth", "col"), "row"), P("row", "col"), P(("depth", "row"), "col"))
    return jax.shard_map(
        on_device,
        mesh=mesh,
        in_specs=placed,
        out_specs=(
            P(("depth", "row"), "col"),
            P(("depth", "col"), "row"),
            P("row", ("col", "depth")),
        ),
        check_vma=False,
    )
```

```python
import jax
import jax.numpy as jnp
from jax import lax
from jax.sharding import PartitionSpec as P

coeff = 0.7978845608
cubic = 0.044715
HALVES = (0, 1)


def gelu_both(hidden):
    square = hidden * hidden
    inner = jnp.tanh(coeff * (hidden + cubic * hidden * square))
    value = 0.5 * hidden * (1.0 + inner)
    slope = 0.5 * (1.0 + inner) + 0.5 * hidden * (1.0 - inner * inner) * coeff * (
        1.0 + 3.0 * cubic * square
    )
    return value, slope


def shift(x, k):
    return lax.ppermute(x, "row", [(i, (i + k) % 8) for i in range(8)])


def x_shift(x, k):
    return lax.ppermute(
        x, "col", [(y * 4 + i, y * 4 + (i + k) % 4) for y in range(2) for i in range(4)]
    )


def y_swap(x):
    return lax.ppermute(x, "col", [(i, (i + 4) % 8) for i in range(8)])


def after(x, *earlier):
    return lax.optimization_barrier((x, *earlier))[0]


def pick(panel, index):
    return lax.dynamic_index_in_dim(panel, index, 0, keepdims=False)


def reduce_lane(first, rest, sign):
    far, near = yield (first[0], sign), (first[1], -sign)
    term = rest()
    for k in (3, 2, 1):
        far = (far.astype(jnp.float32) + term(k * sign)).astype(jnp.bfloat16)
        if k > 1:
            near = (near.astype(jnp.float32) + term((1 - k) * sign)).astype(jnp.bfloat16)
            far, near = yield (far, sign), (near, -sign)
        else:
            (far,) = yield ((far, sign),)
    return far.astype(jnp.float32) + near.astype(jnp.float32) + term(0)


def gather_lane(own, sign):
    blocks = [own] + [None] * 7
    far = near = own
    for k in (1, 2, 3):
        far, near = yield (far, sign), (near, -sign)
        blocks[(-k * sign) % 8], blocks[(k * sign) % 8] = far, near
    (far,) = yield ((far, sign),)
    blocks[4] = far
    return jnp.stack(blocks)


def take_turns(lanes):
    mark, coming = (), [None] * len(lanes)
    lanes = list(lanes)
    while any(lane is not None for lane in lanes):
        for n, lane in enumerate(lanes):
            if lane is None:
                continue
            got = coming[n]
            try:
                if got is None:
                    sends = next(lane)
                else:
                    got = lax.optimization_barrier((got, mark))[0]
                    sends = lane.send(got)
            except StopIteration:
                lanes[n] = None
                continue
            values = tuple(v for v, _ in sends)
            mark = lax.optimization_barrier((values, mark if got is None else got))[0]
            coming[n] = tuple(shift(v, k) for v, (_, k) in zip(mark, sends))


def on_device(tokens, up_weight, grad_out):
    f32, bf16 = jnp.float32, jnp.bfloat16
    row, col, depth = (lax.axis_index(a) for a in ("row", "col", "depth"))
    core, high = depth & 1, depth >> 1
    here, below = core == 0, high == 0
    rows = tokens.shape[0] // 2
    quarter = up_weight.shape[1] // 4

    def place(block):
        return ((block - col) & 3) * 2 + ((block ^ col) >> 2)

    def gather_tokens(own):
        other = y_swap(own)
        ahead, behind = x_shift(own, -1), x_shift(own, 1)
        other, ahead, behind = lax.optimization_barrier((other, ahead, behind))
        far, other_ahead, other_behind = x_shift(ahead, -1), x_shift(other, -1), x_shift(other, 1)
        other_far = x_shift(other_behind, 1)
        blocks = own, other, ahead, other_ahead, far, other_far, behind, other_behind
        return jnp.stack(blocks)

    def product(panel, weight):
        return lax.dot_general(
            panel, weight, (((2,), (0,)), ((), ())), preferred_element_type=f32
        )

    def back_product(h, *earlier):
        blocks = after(gathered[h], *earlier)
        return sum(
            lax.dot_general(
                blocks[:, d],
                up_weight[:, d * quarter : (d + 1) * quarter],
                (((2,), (1,)), ((), ())),
                preferred_element_type=f32,
            )
            for d in range(4)
        )

    panel = gather_tokens(tokens)
    grads, values, gathered, lefts, extra = {}, {}, {}, {}, {}

    def half(x, h, axis=0):
        return lax.slice_in_dim(x, h * rows, (h + 1) * rows, axis=axis)

    def forward(h, sign):
        blocks = half(panel, h, 1)
        if h:
            blocks = after(blocks, *extra["first"])
        chosen = jnp.stack([pick(blocks, place((row + k) & 7)) for k in (4 * sign, -3 * sign)])
        first = product(chosen, up_weight).astype(bf16)
        extra["first"] = first = [first[0], first[1]]

        def rest():
            terms = product(after(blocks, *first), up_weight)
            return lambda k: pick(terms, place((row + k) & 7))

        hidden = yield from reduce_lane(first, rest, sign)
        value, slope = gelu_both(hidden)
        grad = (half(grad_out, h).astype(f32) * slope).astype(bf16)
        values[h] = value.astype(bf16)
        grads[h] = jnp.stack([grad[:, d * quarter : (d + 1) * quarter] for d in range(4)])

    def backward(c, sign, hooks=None):
        gathered[c] = yield from hooked(gather_lane(grads[c], sign), hooks or {})

    def hooked(inner, hooks):
        step, sends = 0, next(inner)
        while True:
            got = yield sends
            step += 1
            if step in hooks:
                got = after(got, *hooks[step]())
            try:
                sends = inner.send(got)
            except StopIteration as stop:
                return stop.value

    def lane(*steps):
        for step in steps:
            yield from step

    def token_rows():
        left = jnp.stack([pick(panel, place((row + m) & 7)) for m in range(8)])
        for h in HALVES:
            chosen = half(left, h, 1)
            lefts[h] = chosen.reshape(-1, chosen.shape[2])
        return list(lefts.values())

    def outer(d, *earlier):
        total = 0
        for h in HALVES:
            cols = lax.dynamic_index_in_dim(after(gathered[h], *earlier), d, 1, keepdims=False)
            total = total + lax.dot_general(
                lefts[h],
                cols.reshape(-1, cols.shape[2]),
                (((0,), (0,)), ((), ())),
                preferred_element_type=f32,
            )
        return total

    def from_core(x):
        return lax.ppermute(x, "depth", [(0, 1), (1, 0), (2, 3), (3, 2)])

    across = (2 * (1 - high) + 1 - core, 2 * (1 - high) + core, 2 * high + 1 - core, depth)

    def token_sends(partial):
        pairs = partial.reshape(2, 4, rows, -1)

        def towards(k):
            return lax.dynamic_index_in_dim(pairs, (col + k - row) & 3, 1, keepdims=False)

        sends = lax.optimization_barrier([towards(k).astype(bf16) for k in (1, 2, 3)])
        return towards(0), sends, [x_shift(v, k) for k, v in zip((1, 2, 3), sends)]

    def token_total(own, got):
        return sum((v.astype(f32) for v in got), own)

    kept = (((row + ((col - row) & 3)) ^ col) >> 2) & 1

    def finish_tokens(total):
        other = y_swap(pick(total, 1 - kept).astype(bf16))
        return (pick(total, kept) + other.astype(f32)).astype(bf16)

    def rows_ready():
        extra["activated"] = jnp.concatenate([values[0], values[1]], 0)
        return [*token_rows(), extra["activated"]]

    lane_a = lane(forward(0, 1), backward(0, 1))
    lane_b = lane(forward(1, -1), backward(1, -1, {2: rows_ready}))
    take_turns([lane_a, lane_b])

    sent = outer(across[0]).astype(bf16)
    away = (outer(across[1], sent) + from_core(sent).astype(f32)).astype(bf16)
    back = lax.ppermute(away, "depth", [(0, 2), (1, 3), (2, 0), (3, 1)])
    own_0, sends_0, got_0 = token_sends(back_product(0, away))
    own_1, sends_1, got_1 = token_sends(back_product(1, *sends_0))
    sent = outer(across[2], *sends_1).astype(bf16)
    mine = outer(across[3], sent) + from_core(sent).astype(f32)
    grad_tokens = [finish_tokens(token_total(*v)) for v in ((own_0, got_0), (own_1, got_1))]
    late = (mine + back.astype(f32)).astype(bf16)

    return (
        extra["activated"],
        jnp.concatenate(grad_tokens, 0),
        late,
    )

def solution(mesh):
    placed = (P(("depth", "col"), "row"), P("row", "col"), P(("depth", "row"), "col"))
    return jax.shard_map(
        on_device,
        mesh=mesh,
        in_specs=placed,
        out_specs=(
            P(("depth", "row"), "col"),
            P(("depth", "col"), "row"),
            P("row", ("col", "depth")),
        ),
        check_vma=False,
    )
```

```python
import jax
import jax.numpy as jnp
from jax import lax
from jax.sharding import PartitionSpec as P

coeff = 0.7978845608
cubic = 0.044715
HALVES = (0, 1)

def gelu_both(hidden):
    square = hidden * hidden
    inner = jnp.tanh(coeff * (hidden + cubic * hidden * square))
    value = 0.5 * hidden * (1.0 + inner)
    slope = 0.5 * (1.0 + inner) + 0.5 * hidden * (1.0 - inner * inner) * coeff * (
        1.0 + 3.0 * cubic * square
    )
    return value, slope

def shift(x, k):
    return lax.ppermute(x, "row", [(i, (i + k) % 8) for i in range(8)])

def x_shift(x, k):
    return lax.ppermute(
        x, "col", [(y * 4 + i, y * 4 + (i + k) % 4) for y in range(2) for i in range(4)]
    )

def y_swap(x):
    return lax.ppermute(x, "col", [(i, (i + 4) % 8) for i in range(8)])

def after(x, *earlier):
    return lax.optimization_barrier((x, *earlier))[0]

def pick(panel, index):
    return lax.dynamic_index_in_dim(panel, index, 0, keepdims=False)

def reduce_lane(first, rest, sign):
    far, near = yield (first[0], sign), (first[1], -sign)
    term = rest()
    for k in (3, 2, 1):
        far = (far.astype(jnp.float32) + term(k * sign)).astype(jnp.bfloat16)
        if k > 1:
            near = (near.astype(jnp.float32) + term((1 - k) * sign)).astype(jnp.bfloat16)
            far, near = yield (far, sign), (near, -sign)
        else:
            (far,) = yield ((far, sign),)
    return far.astype(jnp.float32) + near.astype(jnp.float32) + term(0)

def gather_lane(own, sign):
    blocks = [own] + [None] * 7
    far = near = own
    for k in (1, 2, 3):
        far, near = yield (far, sign), (near, -sign)
        blocks[(-k * sign) % 8], blocks[(k * sign) % 8] = far, near
    (far,) = yield ((far, sign),)
    blocks[4] = far
    return jnp.stack(blocks)

def take_turns(lanes):
    mark, coming = (), [None] * len(lanes)
    lanes = list(lanes)
    while any(lane is not None for lane in lanes):
        for n, lane in enumerate(lanes):
            if lane is None:
                continue
            got = coming[n]
            try:
                if got is None:
                    sends = next(lane)
                else:
                    got = lax.optimization_barrier((got, mark))[0]
                    sends = lane.send(got)
            except StopIteration:
                lanes[n] = None
                continue
            values = tuple(v for v, _ in sends)
            mark = lax.optimization_barrier((values, mark if got is None else got))[0]
            coming[n] = tuple(shift(v, k) for v, (_, k) in zip(mark, sends))

def on_device(tokens, up_weight, grad_out):
    f32, bf16 = jnp.float32, jnp.bfloat16
    row, col, depth = (lax.axis_index(a) for a in ("row", "col", "depth"))
    core, high = depth & 1, depth >> 1
    rows = tokens.shape[0] // 2
    quarter = up_weight.shape[1] // 4

    def place(block):
        return ((block - col) & 3) * 2 + ((block ^ col) >> 2)

    def gather_tokens(own):
        other = y_swap(own)
        ahead, behind = x_shift(own, -1), x_shift(own, 1)
        other, ahead, behind = lax.optimization_barrier((other, ahead, behind))
        far, other_ahead, other_behind = x_shift(ahead, -1), x_shift(other, -1), x_shift(other, 1)
        other_far = x_shift(other_behind, 1)
        blocks = own, other, ahead, other_ahead, far, other_far, behind, other_behind
        return jnp.stack(blocks)

    def product(panel, weight):
        return lax.dot_general(
            panel, weight, (((2,), (0,)), ((), ())), preferred_element_type=f32
        )

    def back_product(h, *earlier):
        blocks = after(gathered[h], *earlier)
        return sum(
            lax.dot_general(
                blocks[:, d],
                up_weight[:, d * quarter : (d + 1) * quarter],
                (((2,), (1,)), ((), ())),
                preferred_element_type=f32,
            )
            for d in range(4)
        )

    panel = gather_tokens(tokens)
    grads, values, gathered, lefts, extra = {}, {}, {}, {}, {}

    def half(x, h, axis=0):
        return lax.slice_in_dim(x, h * rows, (h + 1) * rows, axis=axis)

    def forward(h, sign):
        blocks = half(panel, h, 1)
        if h:
            blocks = after(blocks, *extra["first"])
        chosen = jnp.stack([pick(blocks, place((row + k) & 7)) for k in (4 * sign, -3 * sign)])
        first = product(chosen, up_weight).astype(bf16)
        extra["first"] = first = [first[0], first[1]]

        def rest():
            terms = product(after(blocks, *first), up_weight)
            return lambda k: pick(terms, place((row + k) & 7))

        hidden = yield from reduce_lane(first, rest, sign)
        value, slope = gelu_both(hidden)
        grad = (half(grad_out, h).astype(f32) * slope).astype(bf16)
        values[h] = value.astype(bf16)
        grads[h] = jnp.stack([grad[:, d * quarter : (d + 1) * quarter] for d in range(4)])

    def backward(h, sign):
        gathered[h] = yield from gather_lane(grads[h], sign)

    def lane(*steps):
        for step in steps:
            yield from step

    def token_rows():
        left = jnp.stack([pick(panel, place((row + m) & 7)) for m in range(8)])
        return [half(left, h, 1).reshape(8 * rows, -1) for h in HALVES]

    def outer(d, *earlier):
        total = 0
        for h in HALVES:
            cols = lax.dynamic_index_in_dim(after(gathered[h], *earlier), d, 1, keepdims=False)
            total = total + lax.dot_general(
                lefts[h],
                cols.reshape(-1, cols.shape[2]),
                (((0,), (0,)), ((), ())),
                preferred_element_type=f32,
            )
        return total

    def from_core(x):
        return lax.ppermute(x, "depth", [(0, 1), (1, 0), (2, 3), (3, 2)])

    across = (2 * (1 - high) + 1 - core, 2 * (1 - high) + core, 2 * high + 1 - core, depth)

    def token_sends(partial):
        pairs = partial.reshape(2, 4, rows, -1)

        def towards(k):
            return lax.dynamic_index_in_dim(pairs, (col + k - row) & 3, 1, keepdims=False)

        sends = lax.optimization_barrier([towards(k).astype(bf16) for k in (1, 2, 3)])
        return towards(0), sends, [x_shift(v, k) for k, v in zip((1, 2, 3), sends)]

    def token_total(own, got):
        return sum((v.astype(f32) for v in got), own)

    kept = (((row + ((col - row) & 3)) ^ col) >> 2) & 1

    lefts.update(enumerate(token_rows()))
    take_turns([lane(forward(0, 1), backward(0, 1)), lane(forward(1, -1), backward(1, -1))])

    sent = outer(across[0]).astype(bf16)
    away = lax.optimization_barrier(outer(across[1], sent))
    away = (away + from_core(sent).astype(f32)).astype(bf16)
    back = lax.ppermute(away, "depth", [(0, 2), (1, 3), (2, 0), (3, 1)])
    own_0, sends_0, got_0 = token_sends(back_product(0, away))
    own_1, sends_1, got_1 = token_sends(back_product(1, *sends_0))
    got_0 = after(got_0, *sends_1)
    sent = outer(across[2], got_0[0]).astype(bf16)
    mine = outer(across[3], sent) + from_core(sent).astype(f32)
    totals = token_total(own_0, got_0), token_total(own_1, got_1)
    totals = after(totals, back)
    grad_weight = (mine + back.astype(f32)).astype(bf16)
    mine, other = (
        jnp.concatenate([pick(t, n) for t in totals], 0) for n in (kept, 1 - kept)
    )
    other = after(y_swap(other.astype(bf16)), grad_weight)
    grad_tokens = (mine + other.astype(f32)).astype(bf16)

    return (
        jnp.concatenate([values[h] for h in HALVES], 0),
        grad_tokens,
        grad_weight,
    )

def solution(mesh):
    placed = (P(("depth", "col"), "row"), P("row", "col"), P(("depth", "row"), "col"))
    return jax.shard_map(
        on_device,
        mesh=mesh,
        in_specs=placed,
        out_specs=(
            P(("depth", "row"), "col"),
            P(("depth", "col"), "row"),
            P("row", ("col", "depth")),
        ),
        check_vma=False,
    )
```

```python
import jax
import jax.numpy as jnp
from jax import lax
from jax.sharding import PartitionSpec as P

coeff = 0.7978845608
cubic = 0.044715
HALVES = (0, 1)

def gelu_both(hidden):
    square = hidden * hidden
    inner = jnp.tanh(coeff * (hidden + cubic * hidden * square))
    value = 0.5 * hidden * (1.0 + inner)
    slope = 0.5 * (1.0 + inner) + 0.5 * hidden * (1.0 - inner * inner) * coeff * (
        1.0 + 3.0 * cubic * square
    )
    return value, slope

def shift(x, k):
    return lax.ppermute(x, "row", [(i, (i + k) % 8) for i in range(8)])

def x_shift(x, k):
    return lax.ppermute(
        x, "col", [(y * 4 + i, y * 4 + (i + k) % 4) for y in range(2) for i in range(4)]
    )

def y_swap(x):
    return lax.ppermute(x, "col", [(i, (i + 4) % 8) for i in range(8)])

def after(x, *earlier):
    return lax.optimization_barrier((x, *earlier))[0]

def pick(panel, index):
    return lax.dynamic_index_in_dim(panel, index, 0, keepdims=False)

def reduce_lane(first, rest, sign):
    far, near = yield (first[0], sign), (first[1], -sign)
    term = rest()
    for k in (3, 2, 1):
        far = (far.astype(jnp.float32) + term(k * sign)).astype(jnp.bfloat16)
        if k > 1:
            near = (near.astype(jnp.float32) + term((1 - k) * sign)).astype(jnp.bfloat16)
            far, near = yield (far, sign), (near, -sign)
        else:
            (far,) = yield ((far, sign),)
    return far.astype(jnp.float32) + near.astype(jnp.float32) + term(0)

def gather_lane(own, sign):
    blocks = [own] + [None] * 7
    far = near = own
    for k in (1, 2, 3):
        far, near = yield (far, sign), (near, -sign)
        blocks[(-k * sign) % 8], blocks[(k * sign) % 8] = far, near
    (far,) = yield ((far, sign),)
    blocks[4] = far
    return jnp.stack(blocks)

def take_turns(lanes):
    mark, coming = (), [None] * len(lanes)
    lanes = list(lanes)
    while any(lane is not None for lane in lanes):
        for n, lane in enumerate(lanes):
            if lane is None:
                continue
            got = coming[n]
            try:
                if got is None:
                    sends = next(lane)
                else:
                    got = lax.optimization_barrier((got, mark))[0]
                    sends = lane.send(got)
            except StopIteration:
                lanes[n] = None
                continue
            values = tuple(v for v, _ in sends)
            mark = lax.optimization_barrier((values, mark if got is None else got))[0]
            coming[n] = tuple(shift(v, k) for v, (_, k) in zip(mark, sends))

def on_device(tokens, up_weight, grad_out):
    f32, bf16 = jnp.float32, jnp.bfloat16
    row, col, depth = (lax.axis_index(a) for a in ("row", "col", "depth"))
    core, high = depth & 1, depth >> 1
    rows = tokens.shape[0] // 2
    quarter = up_weight.shape[1] // 4

    def place(block):
        return ((block - col) & 3) * 2 + ((block ^ col) >> 2)

    def gather_tokens(own):
        other = y_swap(own)
        ahead, behind, far = [x_shift(own, k) for k in (-1, 1, 2)]
        other_ahead, other_behind = x_shift(other, -1), x_shift(other, 1)
        other_far = y_swap(far)
        blocks = own, other, ahead, other_ahead, far, other_far, behind, other_behind
        return jnp.stack(blocks)

    def product(panel, weight):
        return lax.dot_general(
            panel, weight, (((2,), (0,)), ((), ())), preferred_element_type=f32
        )

    def back_product(h, *earlier):
        blocks = after(gathered[h], *earlier)
        return sum(
            lax.dot_general(
                blocks[:, d],
                up_weight[:, d * quarter : (d + 1) * quarter],
                (((2,), (1,)), ((), ())),
                preferred_element_type=f32,
            )
            for d in range(4)
        )

    panel = gather_tokens(tokens)
    grads, values, gathered, lefts, extra = {}, {}, {}, {}, {}

    def half(x, h, axis=0):
        return lax.slice_in_dim(x, h * rows, (h + 1) * rows, axis=axis)

    def forward(h, sign):
        blocks = half(panel, h, 1)
        if h:
            blocks = after(blocks, *extra["first"])
        chosen = jnp.stack([pick(blocks, place((row + k) & 7)) for k in (4 * sign, -3 * sign)])
        first = product(chosen, up_weight).astype(bf16)
        extra["first"] = first = [first[0], first[1]]

        def rest():
            terms = product(after(blocks, *first), up_weight)
            return lambda k: pick(terms, place((row + k) & 7))

        hidden = yield from reduce_lane(first, rest, sign)
        value, slope = gelu_both(hidden)
        grad = (half(grad_out, h).astype(f32) * slope).astype(bf16)
        values[h] = value.astype(bf16)
        grads[h] = jnp.stack([grad[:, d * quarter : (d + 1) * quarter] for d in range(4)])

    def backward(h, sign):
        gathered[h] = yield from gather_lane(grads[h], sign)

    def lane(*steps):
        for step in steps:
            yield from step

    def token_rows():
        left = jnp.stack([pick(panel, place((row + m) & 7)) for m in range(8)])
        return [half(left, h, 1).reshape(8 * rows, -1) for h in HALVES]

    def outer(d, *earlier):
        total = 0
        for h in HALVES:
            cols = lax.dynamic_index_in_dim(after(gathered[h], *earlier), d, 1, keepdims=False)
            total = total + lax.dot_general(
                lefts[h],
                cols.reshape(-1, cols.shape[2]),
                (((0,), (0,)), ((), ())),
                preferred_element_type=f32,
            )
        return total

    def from_core(x):
        return lax.ppermute(x, "depth", [(0, 1), (1, 0), (2, 3), (3, 2)])

    across = (2 * (1 - high) + 1 - core, 2 * (1 - high) + core, 2 * high + 1 - core, depth)

    def token_sends(partial):
        pairs = partial.reshape(2, 4, rows, -1)

        def towards(k):
            return lax.dynamic_index_in_dim(pairs, (col + k - row) & 3, 1, keepdims=False)

        sends = lax.optimization_barrier([towards(k).astype(bf16) for k in (1, 2, 3)])
        return towards(0), sends, [x_shift(v, k) for k, v in zip((1, 2, 3), sends)]

    def token_total(own, got):
        return sum((v.astype(f32) for v in got), own)

    kept = (((row + ((col - row) & 3)) ^ col) >> 2) & 1

    lefts.update(enumerate(token_rows()))
    take_turns([lane(forward(0, 1), backward(0, 1)), lane(forward(1, -1), backward(1, -1))])

    sent = outer(across[0]).astype(bf16)
    away = lax.optimization_barrier(outer(across[1], sent))
    away = (away + from_core(sent).astype(f32)).astype(bf16)
    back = lax.ppermute(away, "depth", [(0, 2), (1, 3), (2, 0), (3, 1)])
    own_0, sends_0, got_0 = token_sends(back_product(0, away))
    own_1, sends_1, got_1 = token_sends(back_product(1, *sends_0))
    got_0 = after(got_0, *sends_1)
    sent = outer(across[2], got_0[0]).astype(bf16)
    mine = outer(across[3], sent) + from_core(sent).astype(f32)
    totals = token_total(own_0, got_0), token_total(own_1, got_1)
    totals = after(totals, back)
    grad_weight = (mine + back.astype(f32)).astype(bf16)
    mine, other = (
        jnp.concatenate([pick(t, n) for t in totals], 0) for n in (kept, 1 - kept)
    )
    other = after(y_swap(other.astype(bf16)), grad_weight)
    grad_tokens = (mine + other.astype(f32)).astype(bf16)

    return (
        jnp.concatenate([values[h] for h in HALVES], 0),
        grad_tokens,
        grad_weight,
    )

def solution(mesh):
    placed = (P(("depth", "col"), "row"), P("row", "col"), P(("depth", "row"), "col"))
    return jax.shard_map(
        on_device,
        mesh=mesh,
        in_specs=placed,
        out_specs=(
            P(("depth", "row"), "col"),
            P(("depth", "col"), "row"),
            P("row", ("col", "depth")),
        ),
        check_vma=False,
    )
```

```python
import jax
import jax.numpy as jnp
from jax import lax
from jax.sharding import PartitionSpec as P

coeff = 0.7978845608
cubic = 0.044715
HALVES = (0, 1)

def gelu_both(hidden):
    square = hidden * hidden
    inner = jnp.tanh(coeff * (hidden + cubic * hidden * square))
    value = 0.5 * hidden * (1.0 + inner)
    slope = 0.5 * (1.0 + inner) + 0.5 * hidden * (1.0 - inner * inner) * coeff * (
        1.0 + 3.0 * cubic * square
    )
    return value, slope

def shift(x, k):
    return lax.ppermute(x, "row", [(i, (i + k) % 8) for i in range(8)])

def x_shift(x, k):
    return lax.ppermute(
        x, "col", [(y * 4 + i, y * 4 + (i + k) % 4) for y in range(2) for i in range(4)]
    )

def y_swap(x):
    return lax.ppermute(x, "col", [(i, (i + 4) % 8) for i in range(8)])

def after(x, *earlier):
    return lax.optimization_barrier((x, *earlier))[0]

def pick(panel, index):
    return lax.dynamic_index_in_dim(panel, index, 0, keepdims=False)

def reduce_lane(first, rest, sign):
    far, near = yield (first[0], sign), (first[1], -sign)
    term = rest()
    for k in (3, 2, 1):
        far = (far.astype(jnp.float32) + term(k * sign)).astype(jnp.bfloat16)
        if k > 1:
            near = (near.astype(jnp.float32) + term((1 - k) * sign)).astype(jnp.bfloat16)
            far, near = yield (far, sign), (near, -sign)
        else:
            (far,) = yield ((far, sign),)
    return far.astype(jnp.float32) + near.astype(jnp.float32) + term(0)

def gather_lane(own, sign):
    blocks = [own] + [None] * 7
    far = near = own
    for k in (1, 2, 3):
        far, near = yield (far, sign), (near, -sign)
        blocks[(-k * sign) % 8], blocks[(k * sign) % 8] = far, near
    (far,) = yield ((far, sign),)
    blocks[4] = far
    return jnp.stack(blocks)

def take_turns(lanes):
    mark, coming = (), [None] * len(lanes)
    lanes = list(lanes)
    while any(lane is not None for lane in lanes):
        for n, lane in enumerate(lanes):
            if lane is None:
                continue
            got = coming[n]
            try:
                if got is None:
                    sends = next(lane)
                else:
                    got = lax.optimization_barrier((got, mark))[0]
                    sends = lane.send(got)
            except StopIteration:
                lanes[n] = None
                continue
            values = tuple(v for v, _ in sends)
            mark = lax.optimization_barrier((values, mark if got is None else got))[0]
            coming[n] = tuple(shift(v, k) for v, (_, k) in zip(mark, sends))

def on_device(tokens, up_weight, grad_out):
    f32, bf16 = jnp.float32, jnp.bfloat16
    row, col, depth = (lax.axis_index(a) for a in ("row", "col", "depth"))
    core, high = depth & 1, depth >> 1
    rows = tokens.shape[0] // 2
    quarter = up_weight.shape[1] // 4

    def place(block):
        return ((block - col) & 3) * 2 + ((block ^ col) >> 2)

    def gather_tokens(own):
        other = y_swap(own)
        ahead, behind, far = [x_shift(own, k) for k in (-1, 1, 2)]
        other_ahead, other_behind = x_shift(other, -1), x_shift(other, 1)
        other_far = y_swap(far)
        blocks = own, other, ahead, other_ahead, far, other_far, behind, other_behind
        return jnp.stack(blocks)

    def product(panel, weight):
        return lax.dot_general(
            panel, weight, (((2,), (0,)), ((), ())), preferred_element_type=f32
        )

    def back_product(h, *earlier):
        blocks = after(gathered[h], *earlier)
        return sum(
            lax.dot_general(
                blocks[:, d],
                up_weight[:, d * quarter : (d + 1) * quarter],
                (((2,), (1,)), ((), ())),
                preferred_element_type=f32,
            )
            for d in range(4)
        )

    panel = gather_tokens(tokens)
    grads, values, gathered, lefts, extra = {}, {}, {}, {}, {}

    def half(x, h, axis=0):
        return lax.slice_in_dim(x, h * rows, (h + 1) * rows, axis=axis)

    def forward(h, sign):
        blocks = half(panel, h, 1)
        if h:
            blocks = after(blocks, *extra["first"])
        chosen = jnp.stack([pick(blocks, place((row + k) & 7)) for k in (4 * sign, -3 * sign)])
        first = product(chosen, up_weight).astype(bf16)
        extra["first"] = first = [first[0], first[1]]

        def rest():
            terms = product(after(blocks, *first), up_weight)
            return lambda k: pick(terms, place((row + k) & 7))

        hidden = yield from reduce_lane(first, rest, sign)
        value, slope = gelu_both(hidden)
        grad = (half(grad_out, h).astype(f32) * slope).astype(bf16)
        values[h] = value.astype(bf16)
        grads[h] = jnp.stack([grad[:, d * quarter : (d + 1) * quarter] for d in range(4)])

    def backward(h, sign):
        inner, steps = gather_lane(grads[h], sign), 0
        sends = next(inner)
        while h not in gathered:
            got = yield sends
            steps += 1
            if h and steps == 2:
                extra["activated"] = jnp.concatenate([values[n] for n in HALVES], 0)
                got = after(got, extra["activated"][:8, :128])
            try:
                sends = inner.send(got)
            except StopIteration as stop:
                gathered[h] = stop.value

    def lane(*steps):
        for step in steps:
            yield from step

    def token_rows():
        left = jnp.stack([pick(panel, place((row + m) & 7)) for m in range(8)])
        return [half(left, h, 1).reshape(8 * rows, -1) for h in HALVES]

    def outer(d, *earlier):
        total = 0
        for h in HALVES:
            cols = lax.dynamic_index_in_dim(after(gathered[h], *earlier), d, 1, keepdims=False)
            total = total + lax.dot_general(
                lefts[h],
                cols.reshape(-1, cols.shape[2]),
                (((0,), (0,)), ((), ())),
                preferred_element_type=f32,
            )
        return total

    def from_core(x):
        return lax.ppermute(x, "depth", [(0, 1), (1, 0), (2, 3), (3, 2)])

    across = (2 * (1 - high) + 1 - core, 2 * (1 - high) + core, 2 * high + 1 - core, depth)

    def token_sends(partial):
        pairs = partial.reshape(2, 4, rows, -1)

        def towards(k):
            return lax.dynamic_index_in_dim(pairs, (col + k - row) & 3, 1, keepdims=False)

        sends = lax.optimization_barrier([towards(k).astype(bf16) for k in (1, 2, 3)])
        return towards(0), sends, [x_shift(v, k) for k, v in zip((1, 2, 3), sends)]

    def token_total(own, got):
        return sum((v.astype(f32) for v in got), own)

    kept = (((row + ((col - row) & 3)) ^ col) >> 2) & 1

    lefts.update(enumerate(token_rows()))
    take_turns([lane(forward(0, 1), backward(0, 1)), lane(forward(1, -1), backward(1, -1))])

    sent = outer(across[0]).astype(bf16)
    away = lax.optimization_barrier(outer(across[1], sent))
    away = (away + from_core(sent).astype(f32)).astype(bf16)
    back = lax.ppermute(away, "depth", [(0, 2), (1, 3), (2, 0), (3, 1)])
    own_0, sends_0, got_0 = token_sends(back_product(0, away))
    own_1, sends_1, got_1 = token_sends(back_product(1, *sends_0))
    got_0 = after(got_0, *sends_1)
    sent = outer(across[2], got_0[0]).astype(bf16)
    mine = outer(across[3], sent) + from_core(sent).astype(f32)
    totals = token_total(own_0, got_0), token_total(own_1, got_1)
    totals = after(totals, back)
    grad_weight = (mine + back.astype(f32)).astype(bf16)
    mine, other = (
        jnp.concatenate([pick(t, n) for t in totals], 0) for n in (kept, 1 - kept)
    )
    other = after(y_swap(other.astype(bf16)), grad_weight)
    grad_tokens = (mine + other.astype(f32)).astype(bf16)

    return (
        extra["activated"],
        grad_tokens,
        grad_weight,
    )

def solution(mesh):
    placed = (P(("depth", "col"), "row"), P("row", "col"), P(("depth", "row"), "col"))
    return jax.shard_map(
        on_device,
        mesh=mesh,
        in_specs=placed,
        out_specs=(
            P(("depth", "row"), "col"),
            P(("depth", "col"), "row"),
            P("row", ("col", "depth")),
        ),
        check_vma=False,
    )
```
